128 devices in a mesh: image: 4 (over x), context: 16 (over y, z_lo, core), dp: 2 (over z_hi).
Axes of the slice: x: 4, y: 4, z: 4 (z_hi: 2, z_lo: 2; z = z_hi * 2 + z_lo), core: 2. Of those that a mesh axis runs over, the one named last changes fastest.
Arguments:
- text: bfloat16 [8192, 8192], P(('context', 'dp'), 'image'), may hold values from -6 to 6
- patches: bfloat16 [8, 1024, 8192], P('image', ('context', 'dp')), may hold values from -6 to 6
- in_gain: float32 [8192], replicated, may hold values from 0.25 to 1.75
- q_weight: bfloat16 [8192, 4096], P('dp', 'image'), may hold values from -0.0625 to 0.0625
- k_weight: bfloat16 [8192, 512], P('dp', 'image'), may hold values from -0.0625 to 0.0625
- v_weight: bfloat16 [8192, 512], P('dp', 'image'), may hold values from -0.0625 to 0.0625
- o_weight: bfloat16 [4096, 8192], P('image', 'dp'), may hold values from -0.09375 to 0.09375
- q_gain: float32 [128], replicated, may hold values from 1 to 32
- k_gain: float32 [128], replicated, may hold values from 1 to 32
- gate: float32 [1], replicated, may hold values from 0.4 to 1.5
- block_mask: int32 [64, 8], P(('context', 'dp')), may hold values from 0 to 1, as said below
- owner_ids: int32 [8], replicated, may hold values from 0 to 7, each once
Outputs:
- mixed: bfloat16 [8192, 8192], P(('context', 'dp'), 'image')
The draws below stay inside these ranges and needn't reach their ends.
Inputs may be any that keep to these rules, and one draw needn't show every extreme that they name: `block_mask`: every text block reads at least one image. `owner_ids`: a permutation of the image numbers.
All inputs are finite; a program needn't handle non-finite values.
Results may differ from the reference program's by a relative error of at most 0.017.
The reference program's roundings to bfloat16 on the way (of `normed`, `queries`, `weights` and `attended`) count: a program that leaves them out, or rounds other values in their place, can miss the bound.
Values may be sent and summed in bfloat16 or wider, within the bound.
A program may use at most 192 MiB of HBM per device.

```python
import jax
import jax.numpy as jnp
from jax import lax

D = 8192
HQ = 32
KVH = 4
HD = 128
BLOCK = 128
TOKENS = 8192
BLOCKS = 64
IMAGES = 8
P_SIZE = 1024


def gain_draw(key):
    first = jax.random.fold_in(key, 0)
    base = jnp.exp(jax.random.uniform(first, (HD,), jnp.float32, 0.0, jnp.log(4.0)))
    return base


def draw_q_gain(key, part):
    key = jax.random.fold_in(key, 5)
    return gain_draw(key)


def draw_k_gain(key, part):
    key = jax.random.fold_in(key, 6)
    return gain_draw(key)


def draw_block_mask(key, part):
    key = jax.random.fold_in(key, 11)
    first, second = jax.random.split(key)
    common = (jax.random.randint(first, (BLOCKS, IMAGES), 0, 3) == 0).astype(jnp.int32)
    picked = jax.random.randint(second, (BLOCKS,), 0, IMAGES)
    needed = (jnp.arange(IMAGES, dtype=jnp.int32)[None, :] == picked[:, None]).astype(jnp.int32)
    return jnp.maximum(common, needed).astype(jnp.int32)


def level_of(stream_key, extent, cuts, smallest, high):
    level = 1.0
    for position, parts in cuts:
        steps = jax.random.uniform(jax.random.fold_in(jax.random.fold_in(stream_key, 6), position), (parts,), jnp.float32, smallest / len(cuts), high / len(cuts))
        level = level * jnp.repeat(jnp.exp(steps), extent[position] // parts).reshape((-1,) + (1,) * (len(extent) - 1 - position))
    return level


def centred(stream_key, extent, scale, most, cuts=(), held_as=jnp.bfloat16):
    values = jax.random.normal(stream_key, extent, jnp.float32) * scale
    if len(cuts) > 0:
        values = level_of(stream_key, extent, cuts, -0.22, 0.18) * values
    return jnp.clip(values, min=-most, max=most).astype(held_as)


def setup_inputs(seed: int = 0) -> dict:
    key_list = jax.random.split(jax.random.key(seed), 13)
    text = centred(key_list[0], (TOKENS, D), 1.0, 6.0, ((0, 32), (1, 4)))
    patches = centred(key_list[1], (IMAGES, P_SIZE, D), 1.0, 6.0, ((0, 4), (1, 32)))
    in_gain = jnp.clip(1.0 + 0.15 * jax.random.normal(key_list[2], (D,), jnp.float32), 0.25, 1.75)
    q_weight = centred(key_list[3], (D, HQ * HD), D ** -0.5, 0.0625, ((0, 2), (1, 4)))
    k_weight = centred(key_list[4], (D, KVH * HD), D ** -0.5, 0.0625, ((0, 2), (1, 4)))
    v_weight = centred(key_list[5], (D, KVH * HD), D ** -0.5, 0.0625, ((0, 2), (1, 4)))
    o_weight = centred(key_list[6], (HQ * HD, D), (HQ * HD) ** -0.5, 0.09375, ((0, 4), (1, 2)))
    q_gain = draw_q_gain(jax.random.fold_in(key_list[12], 71), 0)
    k_gain = draw_k_gain(jax.random.fold_in(key_list[12], 71), 0)
    gate = jnp.clip(jax.random.uniform(key_list[9], (1,), jnp.float32, 0.4, 1.5), 0.4, 1.5)
    block_mask = draw_block_mask(jax.random.fold_in(key_list[12], 71), 0)
    owner_ids = jax.random.permutation(key_list[11], IMAGES).astype(jnp.int32)
    return {"text": text, "patches": patches, "in_gain": in_gain, "q_weight": q_weight, "k_weight": k_weight, "v_weight": v_weight, "o_weight": o_weight, "q_gain": q_gain, "k_gain": k_gain, "gate": gate, "block_mask": block_mask, "owner_ids": owner_ids}


def rms_scale(values, gain):
    mean_square = lax.optimization_barrier(jnp.mean(values * values, axis=-1, keepdims=True))
    return values * lax.rsqrt(mean_square + 1e-05) * gain

def reference(text, patches, in_gain, q_weight, k_weight, v_weight, o_weight, q_gain, k_gain, gate, block_mask, owner_ids):
    group = HQ // KVH
    normed = rms_scale(text.astype(jnp.float32), in_gain).astype(jnp.bfloat16)
    queries = jnp.dot(normed, q_weight, preferred_element_type=jnp.float32).reshape(TOKENS, HQ, HD)
    queries = rms_scale(queries, q_gain).astype(jnp.bfloat16)
    rows = patches.reshape(IMAGES * P_SIZE, D)
    keys = jnp.dot(rows, k_weight, preferred_element_type=jnp.float32).reshape(IMAGES * P_SIZE, KVH, HD)
    keys = rms_scale(keys, k_gain).astype(jnp.bfloat16).astype(jnp.float32)
    values = jnp.dot(rows, v_weight, preferred_element_type=jnp.float32).astype(jnp.bfloat16)
    values = values.reshape(IMAGES * P_SIZE, KVH, HD).astype(jnp.float32)
    onehot = (owner_ids[:, None] == jnp.arange(IMAGES, dtype=jnp.int32)[None, :]).astype(jnp.int32)
    readable = lax.optimization_barrier(jnp.sum(block_mask[:, None, :] * onehot[None, :, :], axis=2))
    query_blocks = queries.reshape(BLOCKS, BLOCK, KVH, group, HD)
    scale = 1.0 / HD ** 0.5

    def one_block(inputs):
        block_queries, block_read = inputs
        key_mask = jnp.repeat(block_read > 0, P_SIZE)
        scores = jnp.einsum('tjgd,kjd->jgtk', block_queries.astype(jnp.float32), keys, precision=lax.Precision.HIGHEST) * scale
        scores = jnp.where(key_mask[None, None, None, :], scores, -1e+30)
        largest = lax.optimization_barrier(jnp.max(scores, axis=-1, keepdims=True))
        weights = jnp.where(key_mask[None, None, None, :], jnp.exp(scores - largest), 0.0)
        total = lax.optimization_barrier(jnp.sum(weights, axis=-1, keepdims=True))
        rounded = lax.optimization_barrier(weights.astype(jnp.bfloat16)).astype(jnp.float32)
        summed = jnp.einsum('jgtk,kjd->tjgd', rounded, values, precision=lax.Precision.HIGHEST)
        summed = summed / jnp.transpose(total, (2, 0, 1, 3))
        return summed.reshape(BLOCK, HQ * HD).astype(jnp.bfloat16)
    attended = lax.map(one_block, (query_blocks, readable)).reshape(TOKENS, HQ * HD)
    projected = jnp.dot(attended, o_weight, preferred_element_type=jnp.float32)
    mixed = jnp.tanh(gate[0]) * projected
    return mixed.astype(jnp.bfloat16)
```

```python
import functools

import jax
import jax.numpy as jnp
from jax import lax
from jax.experimental import pallas as pl
from jax.experimental.pallas import tpu as pltpu
from jax.sharding import PartitionSpec as P

MESH = pl.DeviceIdType.MESH
BF16 = jnp.bfloat16
F32 = jnp.float32
ANY = pl.BlockSpec(memory_space=pl.ANY)
VMEM = pl.BlockSpec(memory_space=pltpu.VMEM)
D = 8192
HD = 128
BLOCK = 128
EPS = 1e-05
NQ = 4


def place():
    x = lax.axis_index("image")
    ctx = lax.axis_index("context")
    zh = lax.axis_index("dp")
    return x, ctx // 4, zh, (ctx // 2) % 2, ctx % 2


def send(src, dst, ss, rs, dev):
    return pltpu.make_async_remote_copy(
        src_ref=src, dst_ref=dst, send_sem=ss, recv_sem=rs, device_id=dev, device_id_type=MESH
    )


def rms(v, gain):
    ms = jnp.mean(v * v, axis=-1, keepdims=True)
    return v * lax.rsqrt(ms + EPS) * gain


def gather_kernel(
    text, patches, gain, qw, kw, vw, ow, qg, kg,
    q_out, kv, wo,
    raw, tn, pb, wq, wkv, acc, kvacc, kvown, sums,
    loc, sum_s, sum_r, ps, pr, ts, tr, ks, kr, qs, qr, os, orr, gs, gr, hs, hr,
):
    x, y, zh, zl, c = place()
    ctx = lax.axis_index("context")
    z = zh * 2 + zl
    xr, xl, xo = (x + 1) % 4, (x + 3) % 4, (x + 2) % 4
    right, left = {"image": xr}, {"image": xl}
    sib = {"context": ctx + 1 - 2 * c}
    near = {"context": ctx + 2 - 4 * zl}
    cross = {"context": ctx + 2 - 4 * zl, "dp": 1 - zh}
    yr = {"context": ((y + 1) % 4) * 4 + zl * 2 + c}
    yl = {"context": ((y + 3) % 4) * 4 + zl * 2 + c}

    def plane(k, sign):
        ty = (y + sign * (k // 4) + 4) % 4
        tz = (z + sign * (k % 4) + 4) % 4
        return ty * 4 + (tz % 2) * 2 + c, tz // 2

    barrier = pltpu.get_barrier_semaphore()
    for d in (1, 2, 3):
        pl.semaphore_signal(barrier, inc=1, device_id={"image": (x + d) % 4}, device_id_type=MESH)
    pl.semaphore_signal(barrier, inc=1, device_id=sib, device_id_type=MESH)

    def greet(k, carry):
        tc, td = plane(k, 1)
        pl.semaphore_signal(barrier, inc=1, device_id={"context": tc, "dp": td}, device_id_type=MESH)
        return carry

    lax.fori_loop(1, 16, greet, 0)

    own_half = pl.ds(zh * 4096, 4096)
    local = [
        pltpu.make_async_copy(text, raw, loc.at[0]),
        pltpu.make_async_copy(patches, pb.at[pl.ds(x * 64, 64)], loc.at[1]),
        pltpu.make_async_copy(kw, wkv.at[own_half, pl.ds(0, 128)], loc.at[2]),
        pltpu.make_async_copy(vw, wkv.at[own_half, pl.ds(128, 128)], loc.at[3]),
        pltpu.make_async_copy(qw, wq.at[own_half], loc.at[4]),
        pltpu.make_async_copy(ow, wo.at[:, own_half], loc.at[5]),
    ]
    for cp in local:
        cp.start()
    pl.semaphore_wait(barrier, 19)
    sends = []

    def go(cp):
        cp.start()
        sends.append(cp)
        return cp

    def prow(slot, half):
        return pb.at[pl.ds(slot * 64 + half * 32, 32)]

    p_r = [go(send(patches.at[pl.ds(0, 32)], prow(x, 0), ps.at[0], pr.at[0], right))]
    p_l = [go(send(patches.at[pl.ds(32, 32)], prow(x, 1), ps.at[3], pr.at[3], left))]

    other = (1 - zh) * 4096

    def kv_flow(base, a, b, dev):
        rows = pl.ds(base + a * 2048 + b * 1024, 1024)
        return rows

    rows_mine = pl.ds(c * 2048 + zl * 1024, 1024)
    rows_there = pl.ds(zh * 4096 + c * 2048 + zl * 1024, 1024)
    k1 = [
        go(send(kw.at[rows_mine], wkv.at[rows_there, pl.ds(0, 128)], ks.at[0], kr.at[0], cross)),
        go(send(vw.at[rows_mine], wkv.at[rows_there, pl.ds(128, 128)], ks.at[1], kr.at[1], cross)),
    ]
    p_r.append(go(send(patches.at[pl.ds(32, 32)], prow(x, 1), ps.at[1], pr.at[1], right)))
    p_l.append(go(send(patches.at[pl.ds(0, 32)], prow(x, 0), ps.at[4], pr.at[4], left)))

    def orow(cy, p):
        return pl.ds(c * 512 + ((cy + 4) % 4) * 128 + p * 64, 64)

    ocol = pl.ds((1 - zh) * 4096, 4096)
    o1 = go(send(ow.at[orow(y, zl)], wo.at[orow(y, zl), own_half], os.at[0], orr.at[0], cross))

    def wq_rows(h, cc, p, j):
        return pl.ds(h * 4096 + cc * 2048 + p * 1024 + j * (1024 // NQ), 1024 // NQ)

    q1 = [
        go(send(qw.at[wq_rows(0, c, zl, j)], wq.at[wq_rows(zh, c, zl, j)], qs.at[0, j], qr.at[0, j], cross))
        for j in range(NQ)
    ]

    local[0].wait()
    part = jnp.zeros((256, 128), F32)
    for j in range(16):
        t = raw[:, j * 128 : (j + 1) * 128].astype(F32)
        part = part + t * t
    row = jnp.sum(part.T, axis=0, keepdims=True)
    sums[x] = jnp.broadcast_to(row, (8, 256))
    s_cp = [
        go(send(sums.at[x], sums.at[x], sum_s.at[d - 1], sum_r.at[d - 1], {"image": (x + d) % 4}))
        for d in (1, 2, 3)
    ]
    for cp in s_cp:
        cp.wait_recv()
    total = sums[0] + sums[1] + sums[2] + sums[3]
    inv = lax.rsqrt(total[0:1] * (1.0 / D) + EPS)
    inv = jnp.broadcast_to(inv, (128, 256)).T
    for j in range(16):
        t = raw[:, j * 128 : (j + 1) * 128].astype(F32)
        g = gain[pl.ds(x * 16 + j, 1), :]
        tn[x, :, j * 128 : (j + 1) * 128] = (t * inv * g).astype(BF16)

    p_r[0].wait_recv()
    p_r.append(go(send(prow(xl, 0), prow(xl, 0), ps.at[2], pr.at[2], right)))
    p_l[0].wait_recv()
    p_l.append(go(send(prow(xr, 1), prow(xr, 1), ps.at[5], pr.at[5], left)))

    def wkv_at(cc, p, v):
        return wkv.at[pl.ds(other + cc * 2048 + p * 1024, 1024), pl.ds(v * 128, 128)]

    k2, k3 = [], []
    for v in (0, 1):
        k1[v].wait_recv()
        piece = wkv_at(c, 1 - zl, v)
        k2.append(go(send(piece, piece, ks.at[2 + v], kr.at[2 + v], near)))
        k3.append(go(send(piece, piece, ks.at[4 + v], kr.at[4 + v], sib)))

    p_r[1].wait_recv()
    p_l[1].wait_recv()

    def trow(slot, half):
        return tn.at[slot, pl.ds(half * 128, 128)]

    t_r = [go(send(trow(x, 0), trow(x, 0), ts.at[0], tr.at[0], right))]
    t_l = [go(send(trow(x, 1), trow(x, 1), ts.at[3], tr.at[3], left))]
    t_r.append(go(send(trow(x, 1), trow(x, 1), ts.at[1], tr.at[1], right)))
    t_l.append(go(send(trow(x, 0), trow(x, 0), ts.at[4], tr.at[4], left)))

    for v in (0, 1):
        k2[v].wait_recv()
        piece = wkv_at(c, zl, v)
        k3.append(go(send(piece, piece, ks.at[6 + v], kr.at[6 + v], sib)))

    o1.wait_recv()

    def opiece(cy, p):
        return wo.at[orow(cy, p), ocol]

    osib = []

    def oto(cy, p, idx, dev):
        piece = opiece(cy, p)
        return go(send(piece, piece, os.at[idx], orr.at[idx], dev))

    o2 = oto(y, 1 - zl, 1, near)
    o_r = [oto(y, 1 - zl, 2, yr)]
    o_l = [oto(y, 1 - zl, 5, yl)]
    osib.append(oto(y, 1 - zl, 8, sib))

    q2, q3 = [], []

    def q_pass(j):
        q1[j].wait_recv()
        piece = wq.at[wq_rows(1 - zh, c, 1 - zl, j)]
        q2.append(go(send(piece, piece, qs.at[1, j], qr.at[1, j], near)))
        q3.append(go(send(piece, piece, qs.at[2, j], qr.at[2, j], sib)))

    def q_last(j):
        q2[j].wait_recv()
        piece = wq.at[wq_rows(1 - zh, c, zl, j)]
        q3.append(go(send(piece, piece, qs.at[3, j], qr.at[3, j], sib)))

    q_pass(0)

    p_r[2].wait_recv()
    p_l[2].wait_recv()
    for i in (1, 2, 3):
        local[i].wait()
    for cp in k3:
        cp.wait_recv()
    kvacc[...] = jnp.zeros_like(kvacc)

    def kv_step(i, carry):
        cols = pl.ds(pl.multiple_of(i * 1024, 1024), 1024)
        kvacc[...] += jnp.dot(pb[:, cols], wkv[cols, :], preferred_element_type=F32)
        return carry

    lax.fori_loop(0, 8, kv_step, 0)
    keys = rms(kvacc[:, 0:128], kg[...]).astype(BF16)
    kvown[:, :, 0:128] = keys.reshape(8, 32, 128)
    kvown[:, :, 128:256] = kvacc[:, 128:256].astype(BF16).reshape(8, 32, 128)

    def kv_at(cc, d):
        return kv.at[:, pl.ds((cc * 2 + d) * 32, 32), :]

    def kv_send(k):
        tc, td = plane(k, 1)
        return send(kvown, kv_at(ctx, zh), gs.at[k], gr.at[k], {"context": tc, "dp": td})

    def kv_start(k, carry):
        kv_send(k).start()
        return carry

    lax.fori_loop(1, 16, kv_start, 0)
    go(send(kvown, kv_at(ctx, zh), hs.at[0], hr.at[0], sib))
    keep = pltpu.make_async_copy(kvown, kv_at(ctx, zh), loc.at[6])
    keep.start()

    o2.wait_recv()
    o_r.append(oto(y, zl, 3, yr))
    o_l.append(oto(y, zl, 6, yl))
    osib.append(oto(y, zl, 9, sib))
    q_pass(1)
    q_last(0)

    t_r[0].wait_recv()
    t_r.append(go(send(trow(xl, 0), trow(xl, 0), ts.at[2], tr.at[2], right)))
    t_l[0].wait_recv()
    t_l.append(go(send(trow(xr, 1), trow(xr, 1), ts.at[5], tr.at[5], left)))

    o_r[0].wait_recv()
    o_r.append(oto(y - 1, 1 - zl, 4, yr))
    osib.append(oto(y - 1, 1 - zl, 10, sib))
    o_l[0].wait_recv()
    osib.append(oto(y + 1, 1 - zl, 11, sib))
    q_pass(2)
    q_last(1)
    o_r[1].wait_recv()
    osib.append(oto(y - 1, zl, 12, sib))
    o_l[1].wait_recv()
    o_l.append(oto(y + 1, zl, 7, yl))
    osib.append(oto(y + 1, zl, 13, sib))
    q_pass(3)
    q_last(2)

    def kv_pass(k, carry):
        kv_send(k).wait_recv()
        sc, sd = plane(k, -1)
        send(kv_at(sc, sd), kv_at(sc, sd), hs.at[k], hr.at[k], sib).start()
        return carry

    lax.fori_loop(1, 16, kv_pass, 0)
    q_last(3)
    o_r[2].wait_recv()
    osib.append(oto(y - 2, 1 - zl, 14, sib))
    o_l[2].wait_recv()
    osib.append(oto(y + 2, zl, 15, sib))

    local[4].wait()
    for cp in q3:
        cp.wait_recv()

    def project(slot):
        def step(i, carry):
            cols = pl.ds(pl.multiple_of(i * 512, 512), 512)
            rows = pl.ds(pl.multiple_of(slot * 2048 + i * 512, 512), 512)
            acc[...] += jnp.dot(tn[slot, :, cols], wq[rows, :], preferred_element_type=F32)
            return carry

        lax.fori_loop(0, 4, step, 0)

    acc[...] = jnp.zeros_like(acc)
    project(x)
    t_r[1].wait_recv()
    project(xl)
    t_l[1].wait_recv()
    project(xr)
    t_r[2].wait_recv()
    t_l[2].wait_recv()
    project(xo)
    for h in range(8):
        q_out[:, h * HD : (h + 1) * HD] = rms(acc[:, h * HD : (h + 1) * HD], qg[...]).astype(BF16)

    local[5].wait()
    keep.wait()

    def kv_end(k, carry):
        kv_send(k).wait_send()
        return carry

    lax.fori_loop(1, 16, kv_end, 0)

    def sib_end(k, carry):
        sc, sd = plane(k, -1)
        cp = send(kv_at(sc, sd), kv_at(sc, sd), hs.at[k], hr.at[k], sib)
        cp.wait_recv()
        cp.wait_send()
        return carry

    lax.fori_loop(1, 16, sib_end, 0)
    send(kvown, kv_at(ctx, zh), hs.at[0], hr.at[0], sib).wait_recv()
    for cp in osib:
        cp.wait_recv()
    for cp in sends:
        cp.wait_send()


def gather_call(text, patches, in_gain, qw, kw, vw, ow, q_gain, k_gain):
    dma = pltpu.SemaphoreType.DMA
    return pl.pallas_call(
        gather_kernel,
        name="gather_project",
        out_shape=(
            jax.ShapeDtypeStruct((256, 1024), BF16),
            jax.ShapeDtypeStruct((8, 1024, 256), BF16),
            jax.ShapeDtypeStruct((1024, D), BF16),
        ),
        in_specs=[ANY, ANY, VMEM, ANY, ANY, ANY, ANY, VMEM, VMEM],
        out_specs=(VMEM, ANY, ANY),
        scratch_shapes=[
            pltpu.VMEM((256, 2048), BF16),
            pltpu.VMEM((4, 256, 2048), BF16),
            pltpu.VMEM((256, D), BF16),
            pltpu.VMEM((D, 1024), BF16),
            pltpu.VMEM((D, 256), BF16),
            pltpu.VMEM((256, 1024), F32),
            pltpu.VMEM((256, 256), F32),
            pltpu.VMEM((8, 32, 256), BF16),
            pltpu.VMEM((4, 8, 256), F32),
            dma((7,)), dma((3,)), dma((3,)), dma((6,)), dma((6,)), dma((6,)), dma((6,)),
            dma((8,)), dma((8,)), dma((4, NQ)), dma((4, NQ)), dma((16,)), dma((16,)),
            dma((16,)), dma((16,)), dma((16,)), dma((16,)),
        ],
        compiler_params=pltpu.CompilerParams(
            collective_id=0, has_side_effects=True, vmem_limit_bytes=56 << 20
        ),
    )(
        text, patches.reshape(64, D), in_gain.reshape(64, 128), qw, kw, vw, ow,
        q_gain.reshape(1, HD), k_gain.reshape(1, HD),
    )


LOG2E = 1.4426950408889634


def attend_kernel(mask, owner, q, kv, out, qh, m, l, a):
    s = pl.program_id(0)
    image = owner[s]

    @pl.when(s == 0)
    def _():
        m[...] = jnp.full_like(m, -1e30)
        l[...] = jnp.zeros_like(l)
        a[...] = jnp.zeros_like(a)
        for b in range(2):
            for h in range(8):
                qh[b, h * 128 : (h + 1) * 128, :] = q[b * 128 : (b + 1) * 128, h * 128 : (h + 1) * 128]

    scale = LOG2E / HD**0.5
    for b in range(2):

        @pl.when(mask[b, image] > 0)
        def _(b=b):
            keys = kv[0, :, 0:128]
            vals = kv[0, :, 128:256]
            for t in range(4):
                rows = slice(t * 256, (t + 1) * 256)
                sc = lax.dot_general(
                    qh[b, rows, :], keys, (((1,), (1,)), ((), ())), preferred_element_type=F32
                )
                old = m[b, rows, :]
                new = jnp.maximum(old, jnp.max(sc, axis=-1, keepdims=True) * scale)
                w = jnp.exp2(sc * scale - new[:, 0:1])
                fac = jnp.exp2(old - new)
                l[b, rows, :] = l[b, rows, :] * fac + jnp.sum(w, axis=-1, keepdims=True)
                a[b, rows, :] = a[b, rows, :] * fac + jnp.dot(
                    w.astype(BF16), vals, preferred_element_type=F32
                )
                m[b, rows, :] = new

    @pl.when(s == 7)
    def _():
        for b in range(2):
            for h in range(8):
                rows = slice(h * 128, (h + 1) * 128)
                out[b * 128 : (b + 1) * 128, rows] = (a[b, rows, :] / l[b, rows, :]).astype(BF16)


def attend_call(q, kv, mask, owner):
    return pl.pallas_call(
        attend_kernel,
        name="attend",
        out_shape=jax.ShapeDtypeStruct((256, 1024), BF16),
        grid_spec=pltpu.PrefetchScalarGridSpec(
            num_scalar_prefetch=2,
            grid=(8,),
            in_specs=[
                pl.BlockSpec((256, 1024), lambda s, *_: (0, 0)),
                pl.BlockSpec((1, 1024, 256), lambda s, *_: (s, 0, 0)),
            ],
            out_specs=pl.BlockSpec((256, 1024), lambda s, *_: (0, 0)),
            scratch_shapes=[
                pltpu.VMEM((2, 1024, 128), BF16),
                pltpu.VMEM((2, 1024, 128), F32),
                pltpu.VMEM((2, 1024, 128), F32),
                pltpu.VMEM((2, 1024, 128), F32),
            ],
        ),
        compiler_params=pltpu.CompilerParams(vmem_limit_bytes=48 << 20),
    )(mask, owner, q, kv)


def output_kernel(att, wo, gate, out, w, part, give, take, loc, ss, rs):
    x = lax.axis_index("image")
    xr, xl, xo = (x + 1) % 4, (x + 3) % 4, (x + 2) % 4
    right, left = {"image": xr}, {"image": xl}
    order = (xo, xr, xl, x)
    cps = [
        pltpu.make_async_copy(wo.at[:, pl.ds(t * 2048, 2048)], w.at[i], loc.at[i])
        for i, t in enumerate(order)
    ]
    for cp in cps:
        cp.start()
    barrier = pltpu.get_barrier_semaphore()
    for dev in (right, left):
        pl.semaphore_signal(barrier, inc=1, device_id=dev, device_id_type=MESH)
    pl.semaphore_wait(barrier, 2)

    def product(i, store):
        cps[i].wait()

        def step(n, carry):
            cols = pl.ds(pl.multiple_of(n * 512, 512), 512)
            store(cols, jnp.dot(att[...], w[i, :, cols], preferred_element_type=F32))
            return carry

        lax.fori_loop(0, 4, step, 0)

    def copy(i, dev):
        return send(give.at[i], take.at[i], ss.at[i], rs.at[i], dev)

    def far(cols, v):
        give[0, :, cols] = v[0:128].astype(BF16)
        give[1, :, cols] = v[128:256].astype(BF16)

    product(0, far)
    c0, c1 = copy(0, right), copy(1, left)
    c0.start()
    c1.start()

    def to_right(cols, v):
        give[3, :, cols] = v[128:256].astype(BF16)
        part[0, :, cols] = v[0:128]

    product(1, to_right)
    c3 = copy(3, right)
    c3.start()

    def to_left(cols, v):
        give[4, :, cols] = v[0:128].astype(BF16)
        part[1, :, cols] = v[128:256]

    product(2, to_left)
    c4 = copy(4, left)
    c4.start()

    c0.wait_recv()
    give[2] = (part[0] + take[0].astype(F32)).astype(BF16)
    c2 = copy(2, right)
    c2.start()
    c1.wait_recv()
    give[5] = (part[1] + take[1].astype(F32)).astype(BF16)
    c5 = copy(5, left)
    c5.start()

    def mine(cols, v):
        part[0, :, cols] = v[0:128]
        part[1, :, cols] = v[128:256]

    product(3, mine)
    scale = jnp.tanh(jnp.full((8, 128), gate[0], F32))[0:1, 0:1]
    c3.wait_recv()
    c4.wait_recv()
    c2.wait_recv()
    out[0:128] = (scale * (part[0] + take[2].astype(F32) + take[4].astype(F32))).astype(BF16)
    c5.wait_recv()
    out[128:256] = (scale * (part[1] + take[3].astype(F32) + take[5].astype(F32))).astype(BF16)
    for cp in (c0, c1, c2, c3, c4, c5):
        cp.wait_send()


def output_call(att, wo, gate):
    dma = pltpu.SemaphoreType.DMA
    return pl.pallas_call(
        output_kernel,
        name="output",
        out_shape=jax.ShapeDtypeStruct((256, 2048), BF16),
        in_specs=[VMEM, ANY, pl.BlockSpec(memory_space=pltpu.SMEM)],
        out_specs=VMEM,
        scratch_shapes=[
            pltpu.VMEM((4, 1024, 2048), BF16),
            pltpu.VMEM((2, 128, 2048), F32),
            pltpu.VMEM((6, 128, 2048), BF16),
            pltpu.VMEM((6, 128, 2048), BF16),
            dma((4,)), dma((6,)), dma((6,)),
        ],
        compiler_params=pltpu.CompilerParams(
            collective_id=1, has_side_effects=True, vmem_limit_bytes=48 << 20
        ),
    )(att, wo, gate)


def local(
    text, patches, in_gain, q_weight, k_weight, v_weight, o_weight, q_gain, k_gain, gate, block_mask, owner_ids
):
    q, kv, wo = gather_call(
        text, patches, in_gain, q_weight, k_weight, v_weight, o_weight, q_gain, k_gain
    )
    att = attend_call(q, kv, block_mask, owner_ids)
    return output_call(att, wo, gate)


def solution(mesh):
    in_specs = (
        P(("context", "dp"), "image"),
        P("image", ("context", "dp"), None),
        P(),
        P("dp", "image"),
        P("dp", "image"),
        P("dp", "image"),
        P("image", "dp"),
        P(),
        P(),
        P(),
        P(("context", "dp"), None),
        P(),
    )
    out_specs = P(("context", "dp"), "image")
    return jax.shard_map(local, mesh=mesh, in_specs=in_specs, out_specs=out_specs, check_vma=False)
```

```python
import jax
import jax.numpy as jnp
from jax import lax
from jax.experimental import pallas as pl
from jax.experimental.pallas import tpu as pltpu
from jax.sharding import PartitionSpec as P

MESH = pl.DeviceIdType.MESH
BF16 = jnp.bfloat16
F32 = jnp.float32
ANY = pl.BlockSpec(memory_space=pl.ANY)
VMEM = pl.BlockSpec(memory_space=pltpu.VMEM)
D = 8192
HD = 128
BLOCK = 128
EPS = 1e-05
NQ = 4
HALF = 64
LOG2E = 1.4426950408889634
SCALE = LOG2E / HD**0.5


def place():
    x = lax.axis_index("image")
    ctx = lax.axis_index("context")
    zh = lax.axis_index("dp")
    return x, ctx // 4, zh, (ctx // 2) % 2, ctx % 2


def send(src, dst, ss, rs, dev):
    return pltpu.make_async_remote_copy(
        src_ref=src, dst_ref=dst, send_sem=ss, recv_sem=rs, device_id=dev, device_id_type=MESH
    )


def rms(v, gain):
    ms = jnp.mean(v * v, axis=-1, keepdims=True)
    return v * lax.rsqrt(ms + EPS) * gain


def kernel(
    text, patches, gain, qw, kw, vw, ow, qg, kg, gate, mask, owner,
    out, wo,
    raw, tn, pb, wq, wkv, acc, kvacc, kvb, sums, qh, m, l, a, att, part, give, take,
    loc, wload, sum_s, sum_r, ps, pr, ts, tr, ks, kr, qs, qr, os, orr, gs, gr, hs, hr, rs, rr,
):
    x, y, zh, zl, c = place()
    ctx = lax.axis_index("context")
    z = zh * 2 + zl
    xr, xl, xo = (x + 1) % 4, (x + 3) % 4, (x + 2) % 4
    right, left = {"image": xr}, {"image": xl}
    sib = {"context": ctx + 1 - 2 * c}
    near = {"context": ctx + 2 - 4 * zl}
    cross = {"context": ctx + 2 - 4 * zl, "dp": 1 - zh}

    def at(dy, dz):
        tz = (z + dz + 4) % 4
        return ((y + dy + 4) % 4) * 4 + (tz % 2) * 2 + c, tz // 2

    def to(dy, dz):
        tc, td = at(dy, dz)
        return {"context": tc, "dp": td}

    yr, yl = to(1, 0), to(3, 0)
    barrier = pltpu.get_barrier_semaphore()
    greeted = [{"image": (x + d) % 4} for d in (1, 2, 3)] + [to(d, 0) for d in (1, 2, 3)]
    greeted += [to(0, d) for d in (1, 2, 3)] + [sib]
    for dev in greeted:
        pl.semaphore_signal(barrier, inc=1, device_id=dev, device_id_type=MESH)

    own_half = pl.ds(zh * 4096, 4096)
    local = [
        pltpu.make_async_copy(text, raw, loc.at[0]),
        pltpu.make_async_copy(patches, pb.at[pl.ds(x * 64, 64)], loc.at[1]),
        pltpu.make_async_copy(kw, wkv.at[own_half, pl.ds(0, 128)], loc.at[2]),
        pltpu.make_async_copy(vw, wkv.at[own_half, pl.ds(128, 128)], loc.at[3]),
        pltpu.make_async_copy(qw, wq.at[pl.ds(zh * 4, 4)], loc.at[4]),
    ]
    for cp in local:
        cp.start()
    pl.semaphore_wait(barrier, len(greeted))
    sends = []

    def go(cp):
        cp.start()
        sends.append(cp)
        return cp

    def prow(slot, i):
        return pb.at[pl.ds(slot * 64 + i * 16, 16)]

    def p_first(n):
        p_r.append(go(send(patches.at[pl.ds(n * 16, 16)], prow(x, n), ps.at[n], pr.at[n], right)))
        i = 3 - n
        p_l.append(go(send(patches.at[pl.ds(i * 16, 16)], prow(x, i), ps.at[6 + n], pr.at[6 + n], left)))

    p_r, p_l = [], []
    p_first(0)

    rows_mine = pl.ds(c * 2048 + zl * 1024, 1024)
    rows_there = pl.ds(zh * 4096 + c * 2048 + zl * 1024, 1024)
    k1 = [
        go(send(kw.at[rows_mine], wkv.at[rows_there, pl.ds(0, 128)], ks.at[0], kr.at[0], cross)),
        go(send(vw.at[rows_mine], wkv.at[rows_there, pl.ds(128, 128)], ks.at[1], kr.at[1], cross)),
    ]
    for n in (1, 2, 3):
        p_first(n)

    def orow(cy, p):
        return pl.ds(c * 512 + ((cy + 4) % 4) * 128 + p * 64, 64)

    o1 = go(send(ow.at[orow(y, zl)], wo.at[orow(y, zl)], os.at[0], orr.at[0], cross))

    rows_q = 1024 // NQ

    def wq_at(h, cc, p, j):
        return wq.at[h * 4 + cc * 2 + p, pl.ds(j * rows_q, rows_q)]

    q1 = [
        go(send(qw.at[c * 2 + zl, pl.ds(j * rows_q, rows_q)], wq_at(zh, c, zl, j), qs.at[0, j], qr.at[0, j], cross))
        for j in range(NQ)
    ]

    local[0].wait()
    lanes = jnp.zeros((256, 128), F32)
    for j in range(16):
        t = raw[:, j * 128 : (j + 1) * 128].astype(F32)
        lanes = lanes + t * t
    row = jnp.sum(lanes.T, axis=0, keepdims=True)
    sums[x] = jnp.broadcast_to(row, (8, 256))
    s_cp = [
        go(send(sums.at[x], sums.at[x], sum_s.at[d - 1], sum_r.at[d - 1], {"image": (x + d) % 4}))
        for d in (1, 2, 3)
    ]
    for cp in s_cp:
        cp.wait_recv()
    total = sums[0] + sums[1] + sums[2] + sums[3]
    inv = lax.rsqrt(total[0:1] * (1.0 / D) + EPS)
    inv = jnp.broadcast_to(inv, (128, 256)).T
    for j in range(16):
        t = raw[:, j * 128 : (j + 1) * 128].astype(F32)
        g = gain[pl.ds(x * 16 + j, 1), :]
        tn[x, :, j * 128 : (j + 1) * 128] = (t * inv * g).astype(BF16)

    def p_relay(n):
        p_r[n].wait_recv()
        p_r.append(go(send(prow(xl, n), prow(xl, n), ps.at[4 + n], pr.at[4 + n], right)))
        p_l[n].wait_recv()
        i = 3 - n
        p_l.append(go(send(prow(xr, i), prow(xr, i), ps.at[10 + n], pr.at[10 + n], left)))

    def trow(slot, b, half):
        return tn.at[slot, pl.ds(b * BLOCK + half * HALF, HALF)]

    t_r, t_l = [[], []], [[], []]

    def t_first(b):
        for n in (0, 1):
            piece = trow(x, b, n)
            t_r[b].append(go(send(piece, piece, ts.at[b, n], tr.at[b, n], right)))
            piece = trow(x, b, 1 - n)
            t_l[b].append(go(send(piece, piece, ts.at[b, 3 + n], tr.at[b, 3 + n], left)))

    def t_relay(b):
        t_r[b][0].wait_recv()
        piece = trow(xl, b, 0)
        t_r[b].append(go(send(piece, piece, ts.at[b, 2], tr.at[b, 2], right)))
        t_l[b][0].wait_recv()
        piece = trow(xr, b, 1)
        t_l[b].append(go(send(piece, piece, ts.at[b, 5], tr.at[b, 5], left)))

    def wkv_at(cc, p, v):
        return wkv.at[pl.ds((1 - zh) * 4096 + cc * 2048 + p * 1024, 1024), pl.ds(v * 128, 128)]

    p_relay(0)
    k2, k3 = [], []
    for v in (0, 1):
        k1[v].wait_recv()
        piece = wkv_at(c, 1 - zl, v)
        k2.append(go(send(piece, piece, ks.at[2 + v], kr.at[2 + v], near)))
        k3.append(go(send(piece, piece, ks.at[4 + v], kr.at[4 + v], sib)))
    p_relay(1)
    t_first(0)
    o_sib = []

    def o_to(cy, p, idx, dev):
        piece = wo.at[orow(cy, p)]
        return go(send(piece, piece, os.at[idx], orr.at[idx], dev))

    o1.wait_recv()
    o2 = o_to(y, 1 - zl, 1, near)
    o_r, o_l = [o_to(y, 1 - zl, 2, yr)], [o_to(y, 1 - zl, 5, yl)]
    o_sib.append(o_to(y, 1 - zl, 8, sib))
    for v in (0, 1):
        k2[v].wait_recv()
        piece = wkv_at(c, zl, v)
        k3.append(go(send(piece, piece, ks.at[6 + v], kr.at[6 + v], sib)))

    q2, q3 = [], []

    def q_pass(j):
        q1[j].wait_recv()
        piece = wq_at(1 - zh, c, 1 - zl, j)
        q2.append(go(send(piece, piece, qs.at[1, j], qr.at[1, j], near)))
        q3.append(go(send(piece, piece, qs.at[2, j], qr.at[2, j], sib)))

    def q_last(j):
        q2[j].wait_recv()
        piece = wq_at(1 - zh, c, zl, j)
        q3.append(go(send(piece, piece, qs.at[3, j], qr.at[3, j], sib)))

    q_pass(0)
    o2.wait_recv()
    o_r.append(o_to(y, zl, 3, yr))
    o_l.append(o_to(y, zl, 6, yl))
    o_sib.append(o_to(y, zl, 9, sib))

    for cp in p_r[2:] + p_l[2:] + k3:
        cp.wait_recv()
    for i in (1, 2, 3):
        local[i].wait()
    kvacc[...] = jnp.zeros_like(kvacc)

    def kv_step(i, carry):
        cols = pl.ds(pl.multiple_of(i * 1024, 1024), 1024)
        kvacc[...] += jnp.dot(pb[:, cols], wkv[cols, :], preferred_element_type=F32)
        return carry

    lax.fori_loop(0, 8, kv_step, 0)

    def block(dy, dz):
        sc, sd = at(-dy, -dz)
        return kvb.at[sc * 2 + sd]

    mine = ctx * 2 + zh
    kvb[mine, :, 0:128] = rms(kvacc[:, 0:128], kg[...]).astype(BF16)
    kvb[mine, :, 128:256] = kvacc[:, 128:256].astype(BF16)
    g_cp, h_cp = {}, []

    def g_send(sy, sz, dy, dz):
        piece, k = block(sy, sz), (sy + dy) * 4 + sz + dz
        g_cp[k] = go(send(piece, piece, gs.at[k], gr.at[k], to(dy, dz)))

    def h_send(sy, sz):
        piece, k = block(sy, sz), sy * 4 + sz
        h_cp.append(go(send(piece, piece, hs.at[k], hr.at[k], sib)))

    for dz in (1, 3, 2):
        g_send(0, 0, 0, dz)
    for dy in (1, 3):
        g_send(0, 0, dy, 0)
    h_send(0, 0)

    t_relay(0)
    t_first(1)
    q_pass(1)
    q_last(0)
    for dz in (1, 3, 2):
        g_cp[dz].wait_recv()
        for dy in (1, 3):
            g_send(0, dz, dy, 0)
        h_send(0, dz)
    o_r[0].wait_recv()
    o_r.append(o_to(y - 1, 1 - zl, 4, yr))
    o_sib.append(o_to(y - 1, 1 - zl, 10, sib))
    o_l[0].wait_recv()
    o_sib.append(o_to(y + 1, 1 - zl, 11, sib))
    q_pass(2)
    q_last(1)
    o_r[1].wait_recv()
    o_sib.append(o_to(y - 1, zl, 12, sib))
    o_l[1].wait_recv()
    o_l.append(o_to(y + 1, zl, 7, yl))
    o_sib.append(o_to(y + 1, zl, 13, sib))
    for dz in (0, 1, 3, 2):
        for dy in (1, 3):
            g_cp[dy * 4 + dz].wait_recv()
            if (dy == 1) == (dz < 2):
                g_send(dy, dz, (2 - dy), 0)
            h_send(dy, dz)
    q_pass(3)
    q_last(2)
    q_last(3)
    t_relay(1)

    def project(slot, b):
        def step(i, carry):
            cols = pl.ds(pl.multiple_of(i * 512, 512), 512)
            rows = pl.ds(pl.multiple_of((i % 2) * 512, 512), 512)
            acc[...] += jnp.dot(
                tn[slot, b * BLOCK : (b + 1) * BLOCK, cols], wq[slot * 2 + i // 2, rows, :],
                preferred_element_type=F32,
            )
            return carry

        lax.fori_loop(0, 4, step, 0)

    def queries(b):
        acc[...] = jnp.zeros_like(acc)
        project(x, b)
        t_r[b][1].wait_recv()
        project(xl, b)
        t_l[b][1].wait_recv()
        project(xr, b)
        t_r[b][2].wait_recv()
        t_l[b][2].wait_recv()
        project(xo, b)
        for h in range(8):
            v = rms(acc[:, h * HD : (h + 1) * HD], qg[...])
            qh[b, h * BLOCK : (h + 1) * BLOCK, :] = v.astype(BF16)

    local[4].wait()
    for cp in q3:
        cp.wait_recv()
    queries(0)
    for dz in (0, 1, 3, 2):
        g_cp[8 + dz].wait_recv()
        h_send(2, dz)
    o_r[2].wait_recv()
    o_sib.append(o_to(y - 2, 1 - zl, 14, sib))
    o_l[2].wait_recv()
    o_sib.append(o_to(y + 2, zl, 15, sib))
    for cp in h_cp:
        cp.wait_recv()

    def attend(b, lo, hi):
        if lo == 0:
            m[...] = jnp.full_like(m, -1e30)
            l[...] = jnp.zeros_like(l)
            a[...] = jnp.zeros_like(a)

        def step(s, carry):
            valid = mask[b, owner[s]]
            rows_s = pl.ds(pl.multiple_of(s * 32, 32), 32)

            def scores(t):
                keys = kvb[:, rows_s, 0:128].reshape(1024, 128)
                return lax.dot_general(
                    qh[b, t * 256 : (t + 1) * 256, :], keys, (((1,), (1,)), ((), ())),
                    preferred_element_type=F32,
                )

            after = scores(0)
            for t in range(4):
                rows = slice(t * 256, (t + 1) * 256)
                sc = after
                if t < 3:
                    after = scores(t + 1)
                old = m[rows, :]
                top = jnp.max(sc, axis=-1, keepdims=True) * SCALE
                new = jnp.where(valid > 0, jnp.maximum(old, top), old)
                low = jnp.where(valid > 0, new, 1e30)
                w = jnp.exp2(sc * SCALE - low[:, 0:1])
                fac = jnp.exp2(old - new)
                vals = kvb[:, rows_s, 128:256].reshape(1024, 128)
                l[rows, :] = l[rows, :] * fac + jnp.sum(w, axis=-1, keepdims=True)
                a[rows, :] = a[rows, :] * fac + jnp.dot(w.astype(BF16), vals, preferred_element_type=F32)
                m[rows, :] = new
            return carry

        lax.fori_loop(lo, hi, step, 0)
        if hi == 8:
            for h in range(8):
                rows = slice(h * BLOCK, (h + 1) * BLOCK)
                att[:, h * HD : (h + 1) * HD] = (a[rows, :] / l[rows, :]).astype(BF16)

    def give_to(b, i):
        return send(give.at[b, i], take.at[b, i], rs.at[b, i], rr.at[b, i], left if i in (1, 4, 5) else right)

    r_cp = [{}, {}]

    def product(t, store):
        def step(n, carry):
            cols = pl.ds(pl.multiple_of((n % 2) * 512, 512), 512)
            v = jnp.dot(att[...], wq[t * 2 + n // 2, :, cols], preferred_element_type=F32)
            store(pl.ds(pl.multiple_of(n * 512, 512), 512), v)
            return carry

        lax.fori_loop(0, 4, step, 0)

    def reduce_start(b):
        def far(cols, v):
            give[b, 0, :, cols] = v[0:HALF].astype(BF16)
            give[b, 1, :, cols] = v[HALF:BLOCK].astype(BF16)

        def to_right(cols, v):
            give[b, 3, :, cols] = v[HALF:BLOCK].astype(BF16)
            part[b, 0, :, cols] = v[0:HALF]

        def to_left(cols, v):
            give[b, 4, :, cols] = v[0:HALF].astype(BF16)
            part[b, 1, :, cols] = v[HALF:BLOCK]

        for t, store, slots in ((xo, far, (0, 1)), (xr, to_right, (3,)), (xl, to_left, (4,))):
            product(t, store)
            for i in slots:
                r_cp[b][i] = go(give_to(b, i))

    def reduce_relay(b):
        for k, i in ((0, 2), (1, 5)):
            r_cp[b][k].wait_recv()
            give[b, i] = (part[b, k] + take[b, k].astype(F32)).astype(BF16)
            r_cp[b][i] = go(give_to(b, i))

    def own_product(b):
        def store(cols, v):
            part[b, 0, :, cols] = v[0:HALF]
            part[b, 1, :, cols] = v[HALF:BLOCK]

        product(x, store)

    def finish(b):
        scale = jnp.tanh(jnp.full((8, 128), gate[0], F32))[0:1, 0:1]
        for k, (i, j) in enumerate(((4, 2), (3, 5))):
            r_cp[b][i].wait_recv()
            r_cp[b][j].wait_recv()
            v = part[b, k] + take[b, i].astype(F32) + take[b, j].astype(F32)
            out[b * BLOCK + k * HALF : b * BLOCK + (k + 1) * HALF] = (scale * v).astype(BF16)

    attend(0, 0, 4)
    queries(1)
    for cp in o_sib:
        cp.wait_recv()
    for cp in sends:
        cp.wait_send()
    sends.clear()
    loads = []
    for i in range(4):
        cols = pl.ds(i * 1024, 1024)
        loads.append(pltpu.make_async_copy(ow.at[:, cols], wq.at[zh * 4 + i], wload.at[i]))
        loads.append(pltpu.make_async_copy(wo.at[:, cols], wq.at[(1 - zh) * 4 + i], wload.at[4 + i]))
    for cp in loads:
        cp.start()
    attend(0, 4, 8)
    for cp in loads:
        cp.wait()
    reduce_start(0)
    attend(1, 0, 4)
    reduce_relay(0)
    own_product(0)
    attend(1, 4, 8)
    reduce_start(1)
    finish(0)
    reduce_relay(1)
    own_product(1)
    finish(1)
    for cp in sends:
        cp.wait_send()


def local(
    text, patches, in_gain, q_weight, k_weight, v_weight, o_weight, q_gain, k_gain, gate, block_mask, owner_ids
):
    dma = pltpu.SemaphoreType.DMA
    smem = pl.BlockSpec(memory_space=pltpu.SMEM)
    return pl.pallas_call(
        kernel,
        name="gated_cross_attention",
        out_shape=(
            jax.ShapeDtypeStruct((256, 2048), BF16),
            jax.ShapeDtypeStruct((1024, 4096), BF16),
        ),
        in_specs=[ANY, ANY, VMEM, ANY, ANY, ANY, ANY, VMEM, VMEM, smem, smem, smem],
        out_specs=(VMEM, ANY),
        scratch_shapes=[
            pltpu.VMEM((256, 2048), BF16),
            pltpu.VMEM((4, 256, 2048), BF16),
            pltpu.VMEM((256, D), BF16),
            pltpu.VMEM((8, 1024, 1024), BF16),
            pltpu.VMEM((D, 256), BF16),
            pltpu.VMEM((BLOCK, 1024), F32),
            pltpu.VMEM((256, 256), F32),
            pltpu.VMEM((32, 256, 256), BF16),
            pltpu.VMEM((4, 8, 256), F32),
            pltpu.VMEM((2, 1024, HD), BF16),
            pltpu.VMEM((1024, HD), F32),
            pltpu.VMEM((1024, HD), F32),
            pltpu.VMEM((1024, HD), F32),
            pltpu.VMEM((BLOCK, 1024), BF16),
            pltpu.VMEM((2, 2, HALF, 2048), F32),
            pltpu.VMEM((2, 6, HALF, 2048), BF16),
            pltpu.VMEM((2, 6, HALF, 2048), BF16),
            dma((5,)), dma((8,)), dma((3,)), dma((3,)), dma((12,)), dma((12,)), dma((2, 6)), dma((2, 6)),
            dma((8,)), dma((8,)), dma((4, NQ)), dma((4, NQ)), dma((16,)), dma((16,)),
            dma((16,)), dma((16,)), dma((16,)), dma((16,)), dma((2, 6)), dma((2, 6)),
        ],
        compiler_params=pltpu.CompilerParams(
            collective_id=0, has_side_effects=True, vmem_limit_bytes=60 << 20
        ),
    )(
        text, patches.reshape(64, D), in_gain.reshape(64, 128), q_weight.reshape(4, 1024, 1024), k_weight, v_weight,
        o_weight, q_gain.reshape(1, HD), k_gain.reshape(1, HD), gate, block_mask, owner_ids,
    )[0]


def solution(mesh):
    in_specs = (
        P(("context", "dp"), "image"),
        P("image", ("context", "dp"), None),
        P(),
        P("dp", "image"),
        P("dp", "image"),
        P("dp", "image"),
        P("image", "dp"),
        P(),
        P(),
        P(),
        P(("context", "dp"), None),
        P(),
    )
    out_specs = P(("context", "dp"), "image")
    return jax.shard_map(local, mesh=mesh, in_specs=in_specs, out_specs=out_specs, check_vma=False)
```

```python
import jax
import jax.numpy as jnp
from jax import lax
from jax.experimental import pallas as pl
from jax.experimental.pallas import tpu as pltpu
from jax.sharding import PartitionSpec as P

MESH = pl.DeviceIdType.MESH
BF16 = jnp.bfloat16
F32 = jnp.float32
ANY = pl.BlockSpec(memory_space=pl.ANY)
VMEM = pl.BlockSpec(memory_space=pltpu.VMEM)
D = 8192
HD = 128
BLOCK = 128
EPS = 1e-05
HALF = 64
LOG2E = 1.4426950408889634
SCALE = LOG2E / HD**0.5


def place():
    x = lax.axis_index("image")
    ctx = lax.axis_index("context")
    zh = lax.axis_index("dp")
    return x, ctx // 4, zh, (ctx // 2) % 2, ctx % 2


def send(src, dst, ss, rs, dev):
    return pltpu.make_async_remote_copy(
        src_ref=src, dst_ref=dst, send_sem=ss, recv_sem=rs, device_id=dev, device_id_type=MESH
    )


def rms(v, gain):
    ms = jnp.mean(v * v, axis=-1, keepdims=True)
    return v * lax.rsqrt(ms + EPS) * gain


def kernel(
    text, patches, gain, qw, kw, vw, ow, qg, kg, gate, mask, owner,
    out, wo,
    raw, tn, pb, wq, wkv, acc, kvacc, kvb, sums, qh, m, l, a, att, part, give, take,
    loc, wload, sum_s, sum_r, ps, pr, ts, tr, ks, kr, qs, qr, ys, yrr, os, orr, gs, gr, hs, hr, rs, rr,
):
    x, y, zh, zl, c = place()
    ctx = lax.axis_index("context")
    z = zh * 2 + zl
    xr, xl, xo = (x + 1) % 4, (x + 3) % 4, (x + 2) % 4
    right, left = {"image": xr}, {"image": xl}
    sib = {"context": ctx + 1 - 2 * c}
    near = {"context": ctx + 2 - 4 * zl}
    cross = {"context": ctx + 2 - 4 * zl, "dp": 1 - zh}

    def at(dy, dz):
        tz = (z + dz + 4) % 4
        return ((y + dy + 4) % 4) * 4 + (tz % 2) * 2 + c, tz // 2

    def to(dy, dz):
        tc, td = at(dy, dz)
        return {"context": tc, "dp": td}

    yr, yl = to(1, 0), to(3, 0)
    barrier = pltpu.get_barrier_semaphore()
    greeted = [{"image": (x + d) % 4} for d in (1, 2, 3)] + [to(d, 0) for d in (1, 2, 3)]
    greeted += [to(0, d) for d in (1, 2, 3)] + [sib]
    for dev in greeted:
        pl.semaphore_signal(barrier, inc=1, device_id=dev, device_id_type=MESH)

    own_half = pl.ds(zh * 4096, 4096)
    local = [
        pltpu.make_async_copy(text, raw, loc.at[0]),
        pltpu.make_async_copy(patches, pb.at[pl.ds(x * 64, 64)], loc.at[1]),
        pltpu.make_async_copy(kw, wkv.at[own_half, pl.ds(0, 128)], loc.at[2]),
        pltpu.make_async_copy(vw, wkv.at[own_half, pl.ds(128, 128)], loc.at[3]),
        pltpu.make_async_copy(qw, wq.at[pl.ds(zh * 4, 4)], loc.at[4]),
    ]
    for cp in local:
        cp.start()
    pl.semaphore_wait(barrier, len(greeted))
    sends = []

    def go(cp):
        cp.start()
        sends.append(cp)
        return cp

    def prow(slot, i):
        return pb.at[pl.ds(slot * 64 + i * 16, 16)]

    def p_first(n):
        p_r.append(go(send(patches.at[pl.ds(n * 16, 16)], prow(x, n), ps.at[n], pr.at[n], right)))
        i = 3 - n
        p_l.append(go(send(patches.at[pl.ds(i * 16, 16)], prow(x, i), ps.at[6 + n], pr.at[6 + n], left)))

    p_r, p_l = [], []
    p_first(0)

    class Round:
        def __init__(self, source, piece, ss, rr):
            self.piece, self.ss, self.rr = piece, ss, rr
            self.first = go(send(source, piece(zh, c, y, zl), ss.at[0], rr.at[0], cross))
            self.r, self.l, self.s = [], [], []

        def on(self, dy, p, idx, dev):
            piece = self.piece(1 - zh, c, (y + dy + 4) % 4, p)
            return go(send(piece, piece, self.ss.at[idx], self.rr.at[idx], dev))

        def crossed(self):
            self.first.wait_recv()
            self.near = self.on(0, 1 - zl, 1, near)
            self.r.append(self.on(0, 1 - zl, 2, yr))
            self.l.append(self.on(0, 1 - zl, 5, yl))
            self.s.append(self.on(0, 1 - zl, 8, sib))

        def neared(self):
            self.near.wait_recv()
            self.r.append(self.on(0, zl, 3, yr))
            self.l.append(self.on(0, zl, 6, yl))
            self.s.append(self.on(0, zl, 9, sib))

        def y_first(self):
            self.r[0].wait_recv()
            self.r.append(self.on(-1, 1 - zl, 4, yr))
            self.s.append(self.on(-1, 1 - zl, 10, sib))
            self.l[0].wait_recv()
            self.s.append(self.on(1, 1 - zl, 11, sib))

        def y_second(self):
            self.l[1].wait_recv()
            self.l.append(self.on(1, zl, 7, yl))
            self.s.append(self.on(1, zl, 13, sib))
            self.r[1].wait_recv()
            self.s.append(self.on(-1, zl, 12, sib))

        def y_far(self):
            self.r[2].wait_recv()
            self.s.append(self.on(-2, 1 - zl, 14, sib))
            self.l[2].wait_recv()
            self.s.append(self.on(2, zl, 15, sib))

        def end(self):
            for cp in self.s:
                cp.wait_recv()

    qy = Round(
        qw.at[c * 2 + zl, pl.ds(512 + y * 128, 128)],
        lambda h, cc, cy, p: wq.at[h * 4 + cc * 2 + p, pl.ds(512 + cy * 128, 128)], ys, yrr,
    )

    rows_mine = pl.ds(c * 2048 + zl * 1024, 1024)
    rows_there = pl.ds(zh * 4096 + c * 2048 + zl * 1024, 1024)
    k1 = [
        go(send(kw.at[rows_mine], wkv.at[rows_there, pl.ds(0, 128)], ks.at[0], kr.at[0], cross)),
        go(send(vw.at[rows_mine], wkv.at[rows_there, pl.ds(128, 128)], ks.at[1], kr.at[1], cross)),
    ]

    def wq_at(h, cc, p, j):
        return wq.at[h * 4 + cc * 2 + p, pl.ds(j * 256, 256)]

    q1 = [
        go(send(qw.at[c * 2 + zl, pl.ds(j * 256, 256)], wq_at(zh, c, zl, j), qs.at[0, j], qr.at[0, j], cross))
        for j in range(2)
    ]

    local[0].wait()
    lanes = jnp.zeros((256, 128), F32)
    for j in range(16):
        t = raw[:, j * 128 : (j + 1) * 128].astype(F32)
        lanes = lanes + t * t
    row = jnp.sum(lanes.T, axis=0, keepdims=True)
    sums[x] = jnp.broadcast_to(row, (8, 256))
    s_cp = [
        go(send(sums.at[x], sums.at[x], sum_s.at[d - 1], sum_r.at[d - 1], {"image": (x + d) % 4}))
        for d in (1, 2, 3)
    ]
    for n in (1, 2, 3):
        p_first(n)

    def p_relay(n):
        p_r[n].wait_recv()
        p_r.append(go(send(prow(xl, n), prow(xl, n), ps.at[4 + n], pr.at[4 + n], right)))
        p_l[n].wait_recv()
        i = 3 - n
        p_l.append(go(send(prow(xr, i), prow(xr, i), ps.at[10 + n], pr.at[10 + n], left)))

    qy.crossed()
    p_relay(0)
    for cp in s_cp:
        cp.wait_recv()
    total = sums[0] + sums[1] + sums[2] + sums[3]
    inv = lax.rsqrt(total[0:1] * (1.0 / D) + EPS)
    inv = jnp.broadcast_to(inv, (128, 256)).T
    for j in range(16):
        t = raw[:, j * 128 : (j + 1) * 128].astype(F32)
        g = gain[pl.ds(x * 16 + j, 1), :]
        tn[x, :, j * 128 : (j + 1) * 128] = (t * inv * g).astype(BF16)

    def trow(slot, b, half):
        return tn.at[slot, pl.ds(b * BLOCK + half * HALF, HALF)]

    t_r, t_l = [[], []], [[], []]

    def t_first(b):
        for n in (0, 1):
            piece = trow(x, b, n)
            t_r[b].append(go(send(piece, piece, ts.at[b, n], tr.at[b, n], right)))
            piece = trow(x, b, 1 - n)
            t_l[b].append(go(send(piece, piece, ts.at[b, 3 + n], tr.at[b, 3 + n], left)))

    def t_relay(b):
        t_r[b][0].wait_recv()
        piece = trow(xl, b, 0)
        t_r[b].append(go(send(piece, piece, ts.at[b, 2], tr.at[b, 2], right)))
        t_l[b][0].wait_recv()
        piece = trow(xr, b, 1)
        t_l[b].append(go(send(piece, piece, ts.at[b, 5], tr.at[b, 5], left)))

    def wkv_at(cc, p, v):
        return wkv.at[pl.ds((1 - zh) * 4096 + cc * 2048 + p * 1024, 1024), pl.ds(v * 128, 128)]

    p_relay(1)
    t_first(0)
    qy.neared()
    k2, k3 = [], []
    for v in (0, 1):
        k1[v].wait_recv()
        piece = wkv_at(c, 1 - zl, v)
        k2.append(go(send(piece, piece, ks.at[2 + v], kr.at[2 + v], near)))
        k3.append(go(send(piece, piece, ks.at[4 + v], kr.at[4 + v], sib)))
    qy.y_first()
    qy.y_second()
    for v in (0, 1):
        k2[v].wait_recv()
        piece = wkv_at(c, zl, v)
        k3.append(go(send(piece, piece, ks.at[6 + v], kr.at[6 + v], sib)))

    q2, q3 = [], []

    def q_pass(j):
        q1[j].wait_recv()
        piece = wq_at(1 - zh, c, 1 - zl, j)
        q2.append(go(send(piece, piece, qs.at[1, j], qr.at[1, j], near)))
        q3.append(go(send(piece, piece, qs.at[2, j], qr.at[2, j], sib)))

    def q_last(j):
        q2[j].wait_recv()
        piece = wq_at(1 - zh, c, zl, j)
        q3.append(go(send(piece, piece, qs.at[3, j], qr.at[3, j], sib)))

    q_pass(0)

    for cp in p_r[2:] + p_l[2:] + k3:
        cp.wait_recv()
    for i in (1, 2, 3):
        local[i].wait()
    kvacc[...] = jnp.zeros_like(kvacc)

    def kv_step(i, carry):
        cols = pl.ds(pl.multiple_of(i * 1024, 1024), 1024)
        kvacc[...] += jnp.dot(pb[:, cols], wkv[cols, :], preferred_element_type=F32)
        return carry

    lax.fori_loop(0, 8, kv_step, 0)

    def block(dy, dz):
        sc, sd = at(-dy, -dz)
        return kvb.at[sc * 2 + sd]

    mine = ctx * 2 + zh
    kvb[mine, :, 0:128] = rms(kvacc[:, 0:128], kg[...]).astype(BF16)
    kvb[mine, :, 128:256] = kvacc[:, 128:256].astype(BF16)
    g_cp, h_cp = {}, []

    def g_send(sy, sz, dy, dz):
        piece, k = block(sy, sz), (sy + dy) * 4 + sz + dz
        g_cp[k] = go(send(piece, piece, gs.at[k], gr.at[k], to(dy, dz)))

    def h_send(sy, sz):
        piece, k = block(sy, sz), sy * 4 + sz
        h_cp.append(go(send(piece, piece, hs.at[k], hr.at[k], sib)))

    for dz in (1, 3, 2):
        g_send(0, 0, 0, dz)
    for dy in (1, 3):
        g_send(0, 0, dy, 0)
    h_send(0, 0)

    t_relay(0)
    t_first(1)
    qy.y_far()
    for dz in (1, 3, 2):
        g_cp[dz].wait_recv()
        for dy in (1, 3):
            g_send(0, dz, dy, 0)
        h_send(0, dz)
    q_last(0)
    q_pass(1)
    wide = Round(
        ow.at[pl.ds(c * 512 + y * 128 + zl * 64, 64)],
        lambda h, cc, cy, p: wo.at[pl.ds(cc * 512 + cy * 128 + p * 64, 64)], os, orr,
    )
    for dz in (0, 1, 3, 2):
        for dy in (1, 3):
            g_cp[dy * 4 + dz].wait_recv()
            if (dy == 1) == (dz < 2):
                g_send(dy, dz, (2 - dy), 0)
            h_send(dy, dz)
    t_relay(1)
    q_last(1)

    def project(slot, b):
        def step(i, carry):
            cols = pl.ds(pl.multiple_of(i * 512, 512), 512)
            rows = pl.ds(pl.multiple_of((i % 2) * 512, 512), 512)
            acc[...] += jnp.dot(
                tn[slot, b * BLOCK : (b + 1) * BLOCK, cols], wq[slot * 2 + i // 2, rows, :],
                preferred_element_type=F32,
            )
            return carry

        lax.fori_loop(0, 4, step, 0)

    def queries(b):
        acc[...] = jnp.zeros_like(acc)
        project(x, b)
        t_r[b][1].wait_recv()
        project(xl, b)
        t_l[b][1].wait_recv()
        project(xr, b)
        t_r[b][2].wait_recv()
        t_l[b][2].wait_recv()
        project(xo, b)
        for h in range(8):
            v = rms(acc[:, h * HD : (h + 1) * HD], qg[...])
            qh[b, h * BLOCK : (h + 1) * BLOCK, :] = v.astype(BF16)

    local[4].wait()
    for cp in q3:
        cp.wait_recv()
    qy.end()
    queries(0)
    wide.crossed()
    for dz in (0, 1, 3, 2):
        g_cp[8 + dz].wait_recv()
        h_send(2, dz)
    wide.neared()
    for cp in h_cp:
        cp.wait_recv()

    def attend(b, lo, hi):
        if lo == 0:
            m[...] = jnp.full_like(m, -1e30)
            l[...] = jnp.zeros_like(l)
            a[...] = jnp.zeros_like(a)

        def step(s, carry):
            valid = mask[b, owner[s]]
            rows_s = pl.ds(pl.multiple_of(s * 32, 32), 32)

            def scores(t):
                keys = kvb[:, rows_s, 0:128].reshape(1024, 128)
                return lax.dot_general(
                    qh[b, t * 256 : (t + 1) * 256, :], keys, (((1,), (1,)), ((), ())),
                    preferred_element_type=F32,
                )

            after = scores(0)
            for t in range(4):
                rows = slice(t * 256, (t + 1) * 256)
                sc = after
                if t < 3:
                    after = scores(t + 1)
                old = m[rows, :]
                top = jnp.max(sc, axis=-1, keepdims=True) * SCALE
                new = jnp.where(valid > 0, jnp.maximum(old, top), old)
                low = jnp.where(valid > 0, new, 1e30)
                w = jnp.exp2(sc * SCALE - low[:, 0:1])
                fac = jnp.exp2(old - new)
                vals = kvb[:, rows_s, 128:256].reshape(1024, 128)
                l[rows, :] = l[rows, :] * fac + jnp.sum(w, axis=-1, keepdims=True)
                a[rows, :] = a[rows, :] * fac + jnp.dot(w.astype(BF16), vals, preferred_element_type=F32)
                m[rows, :] = new
            return carry

        lax.fori_loop(lo, hi, step, 0)
        if hi == 8:
            for h in range(8):
                rows = slice(h * BLOCK, (h + 1) * BLOCK)
                att[b, :, h * HD : (h + 1) * HD] = (a[rows, :] / l[rows, :]).astype(BF16)

    def give_to(b, i):
        return send(give.at[b, i], take.at[b, i], rs.at[b, i], rr.at[b, i], left if i in (1, 4, 5) else right)

    r_cp = [{}, {}]

    def product(b, t, store):
        def step(n, carry):
            cols = pl.ds(pl.multiple_of((n % 2) * 512, 512), 512)
            v = jnp.dot(att[b], wq[t * 2 + n // 2, :, cols], preferred_element_type=F32)
            store(pl.ds(pl.multiple_of(n * 512, 512), 512), v)
            return carry

        lax.fori_loop(0, 4, step, 0)

    def reduce_start(b):
        def far(cols, v):
            give[b, 0, :, cols] = v[0:HALF].astype(BF16)
            give[b, 1, :, cols] = v[HALF:BLOCK].astype(BF16)

        def to_right(cols, v):
            give[b, 3, :, cols] = v[HALF:BLOCK].astype(BF16)
            part[b, 0, :, cols] = v[0:HALF]

        def to_left(cols, v):
            give[b, 4, :, cols] = v[0:HALF].astype(BF16)
            part[b, 1, :, cols] = v[HALF:BLOCK]

        for t, store, slots in ((xo, far, (0, 1)), (xr, to_right, (3,)), (xl, to_left, (4,))):
            product(b, t, store)
            for i in slots:
                r_cp[b][i] = go(give_to(b, i))

    def reduce_relay(b):
        for k, i in ((0, 2), (1, 5)):
            r_cp[b][k].wait_recv()
            give[b, i] = (part[b, k] + take[b, k].astype(F32)).astype(BF16)
            r_cp[b][i] = go(give_to(b, i))

    def own_product(b):
        def store(cols, v):
            part[b, 0, :, cols] = v[0:HALF]
            part[b, 1, :, cols] = v[HALF:BLOCK]

        product(b, x, store)

    def finish(b):
        scale = jnp.tanh(jnp.full((8, 128), gate[0], F32))[0:1, 0:1]
        for k, (i, j) in enumerate(((4, 2), (3, 5))):
            r_cp[b][i].wait_recv()
            r_cp[b][j].wait_recv()
            v = part[b, k] + take[b, i].astype(F32) + take[b, j].astype(F32)
            out[b * BLOCK + k * HALF : b * BLOCK + (k + 1) * HALF] = (scale * v).astype(BF16)

    attend(0, 0, 2)
    wide.y_first()
    attend(0, 2, 4)
    wide.y_second()
    queries(1)
    attend(0, 4, 6)
    wide.y_far()
    attend(0, 6, 8)
    wide.end()
    for cp in sends:
        cp.wait_send()
    sends.clear()
    loads = []
    for i in range(4):
        cols = pl.ds(i * 1024, 1024)
        loads.append(pltpu.make_async_copy(ow.at[:, cols], wq.at[zh * 4 + i], wload.at[i]))
        loads.append(pltpu.make_async_copy(wo.at[:, cols], wq.at[(1 - zh) * 4 + i], wload.at[4 + i]))
    for cp in loads:
        cp.start()
    attend(1, 0, 2)
    for cp in loads:
        cp.wait()
    reduce_start(0)
    attend(1, 2, 4)
    reduce_relay(0)
    own_product(0)
    attend(1, 4, 8)
    reduce_start(1)
    finish(0)
    reduce_relay(1)
    own_product(1)
    finish(1)
    for cp in sends:
        cp.wait_send()


def local(
    text, patches, in_gain, q_weight, k_weight, v_weight, o_weight, q_gain, k_gain, gate, block_mask, owner_ids
):
    dma = pltpu.SemaphoreType.DMA
    smem = pl.BlockSpec(memory_space=pltpu.SMEM)
    return pl.pallas_call(
        kernel,
        name="gated_cross_attention",
        out_shape=(
            jax.ShapeDtypeStruct((256, 2048), BF16),
            jax.ShapeDtypeStruct((1024, 4096), BF16),
        ),
        in_specs=[ANY, ANY, VMEM, ANY, ANY, ANY, ANY, VMEM, VMEM, smem, smem, smem],
        out_specs=(VMEM, ANY),
        scratch_shapes=[
            pltpu.VMEM((256, 2048), BF16),
            pltpu.VMEM((4, 256, 2048), BF16),
            pltpu.VMEM((256, D), BF16),
            pltpu.VMEM((8, 1024, 1024), BF16),
            pltpu.VMEM((D, 256), BF16),
            pltpu.VMEM((BLOCK, 1024), F32),
            pltpu.VMEM((256, 256), F32),
            pltpu.VMEM((32, 256, 256), BF16),
            pltpu.VMEM((4, 8, 256), F32),
            pltpu.VMEM((2, 1024, HD), BF16),
            pltpu.VMEM((1024, HD), F32),
            pltpu.VMEM((1024, HD), F32),
            pltpu.VMEM((1024, HD), F32),
            pltpu.VMEM((2, BLOCK, 1024), BF16),
            pltpu.VMEM((2, 2, HALF, 2048), F32),
            pltpu.VMEM((2, 6, HALF, 2048), BF16),
            pltpu.VMEM((2, 6, HALF, 2048), BF16),
            dma((5,)), dma((8,)), dma((3,)), dma((3,)), dma((12,)), dma((12,)), dma((2, 6)), dma((2, 6)),
            dma((8,)), dma((8,)), dma((4, 2)), dma((4, 2)), dma((16,)), dma((16,)), dma((16,)), dma((16,)),
            dma((16,)), dma((16,)), dma((16,)), dma((16,)), dma((2, 6)), dma((2, 6)),
        ],
        compiler_params=pltpu.CompilerParams(
            collective_id=0, has_side_effects=True, vmem_limit_bytes=60 << 20
        ),
    )(
        text, patches.reshape(64, D), in_gain.reshape(64, 128), q_weight.reshape(4, 1024, 1024), k_weight, v_weight,
        o_weight, q_gain.reshape(1, HD), k_gain.reshape(1, HD), gate, block_mask, owner_ids,
    )[0]


def solution(mesh):
    in_specs = (
        P(("context", "dp"), "image"),
        P("image", ("context", "dp"), None),
        P(),
        P("dp", "image"),
        P("dp", "image"),
        P("dp", "image"),
        P("image", "dp"),
        P(),
        P(),
        P(),
        P(("context", "dp"), None),
        P(),
    )
    out_specs = P(("context", "dp"), "image")
    return jax.shard_map(local, mesh=mesh, in_specs=in_specs, out_specs=out_specs, check_vma=False)
```

```python
import jax
import jax.numpy as jnp
from jax import lax
from jax.experimental import pallas as pl
from jax.experimental.pallas import tpu as pltpu
from jax.sharding import PartitionSpec as P

MESH = pl.DeviceIdType.MESH
BF16 = jnp.bfloat16
F32 = jnp.float32
ANY = pl.BlockSpec(memory_space=pl.ANY)
VMEM = pl.BlockSpec(memory_space=pltpu.VMEM)
D = 8192
HD = 128
BLOCK = 128
EPS = 1e-05
HALF = 64
LOG2E = 1.4426950408889634
SCALE = LOG2E / HD**0.5


def place():
    x = lax.axis_index("image")
    ctx = lax.axis_index("context")
    zh = lax.axis_index("dp")
    return x, ctx // 4, zh, (ctx // 2) % 2, ctx % 2


def send(src, dst, ss, rs, dev):
    return pltpu.make_async_remote_copy(
        src_ref=src, dst_ref=dst, send_sem=ss, recv_sem=rs, device_id=dev, device_id_type=MESH
    )


def rms(v, gain):
    ms = jnp.mean(v * v, axis=-1, keepdims=True)
    return v * lax.rsqrt(ms + EPS) * gain


def kernel(
    text, patches, gain, qw, kw, vw, ow, qg, kg, gate, mask, owner,
    out,
    wo, raw, tn, pb, wq, wkv, acc, kvacc, kvb, sums, qh, m, l, a, att, part, give, take,
    loc, wload, sum_s, sum_r, ps, pr, ts, tr, ks, kr, qs, qr, ys, yrr, zs, zr, os, orr, gs, gr, hs, hr, rs, rr,
):
    x, y, zh, zl, c = place()
    ctx = lax.axis_index("context")
    z = zh * 2 + zl
    xr, xl, xo = (x + 1) % 4, (x + 3) % 4, (x + 2) % 4
    right, left = {"image": xr}, {"image": xl}
    sib = {"context": ctx + 1 - 2 * c}
    near = {"context": ctx + 2 - 4 * zl}
    cross = {"context": ctx + 2 - 4 * zl, "dp": 1 - zh}

    def at(dy, dz):
        tz = (z + dz + 4) % 4
        return ((y + dy + 4) % 4) * 4 + (tz % 2) * 2 + c, tz // 2

    def to(dy, dz):
        tc, td = at(dy, dz)
        return {"context": tc, "dp": td}

    yr, yl = to(1, 0), to(3, 0)
    barrier = pltpu.get_barrier_semaphore()
    greeted = [{"image": (x + d) % 4} for d in (1, 2, 3)] + [to(d, 0) for d in (1, 2, 3)]
    greeted += [to(0, d) for d in (1, 2, 3)] + [sib]
    for dev in greeted:
        pl.semaphore_signal(barrier, inc=1, device_id=dev, device_id_type=MESH)

    own_half = pl.ds(zh * 4096, 4096)
    local = [
        pltpu.make_async_copy(text, raw, loc.at[0]),
        pltpu.make_async_copy(patches, pb.at[pl.ds(x * 64, 64)], loc.at[1]),
        pltpu.make_async_copy(kw, wkv.at[own_half, pl.ds(0, 128)], loc.at[2]),
        pltpu.make_async_copy(vw, wkv.at[own_half, pl.ds(128, 128)], loc.at[3]),
        pltpu.make_async_copy(qw, wq.at[pl.ds(zh * 4, 4)], loc.at[4]),
    ]
    for cp in local:
        cp.start()
    pl.semaphore_wait(barrier, len(greeted))
    sends = []

    def go(cp):
        cp.start()
        sends.append(cp)
        return cp

    def prow(slot, i):
        return pb.at[pl.ds(slot * 64 + i * 16, 16)]

    def p_first(n):
        p_r.append(go(send(patches.at[pl.ds(n * 16, 16)], prow(x, n), ps.at[n], pr.at[n], right)))
        i = 3 - n
        p_l.append(go(send(patches.at[pl.ds(i * 16, 16)], prow(x, i), ps.at[6 + n], pr.at[6 + n], left)))

    p_r, p_l = [], []
    p_first(0)

    class Round:
        def __init__(self, source, piece, ss, rr):
            self.piece, self.ss, self.rr = piece, ss, rr
            self.first = go(send(source, piece(zh, c, y, zl), ss.at[0], rr.at[0], cross))
            self.r, self.l, self.s = [], [], []

        def on(self, dy, p, idx, dev):
            piece = self.piece(1 - zh, c, (y + dy + 4) % 4, p)
            return go(send(piece, piece, self.ss.at[idx], self.rr.at[idx], dev))

        def crossed(self):
            self.first.wait_recv()
            self.near = self.on(0, 1 - zl, 1, near)
            self.r.append(self.on(0, 1 - zl, 2, yr))
            self.l.append(self.on(0, 1 - zl, 5, yl))
            self.s.append(self.on(0, 1 - zl, 8, sib))

        def neared(self):
            self.near.wait_recv()
            self.r.append(self.on(0, zl, 3, yr))
            self.l.append(self.on(0, zl, 6, yl))
            self.s.append(self.on(0, zl, 9, sib))

        def y_first(self):
            self.r[0].wait_recv()
            self.r.append(self.on(-1, 1 - zl, 4, yr))
            self.s.append(self.on(-1, 1 - zl, 10, sib))
            self.l[0].wait_recv()
            self.s.append(self.on(1, 1 - zl, 11, sib))

        def y_second(self):
            self.l[1].wait_recv()
            self.l.append(self.on(1, zl, 7, yl))
            self.s.append(self.on(1, zl, 13, sib))
            self.r[1].wait_recv()
            self.s.append(self.on(-1, zl, 12, sib))

        def y_far(self):
            self.r[2].wait_recv()
            self.s.append(self.on(-2, 1 - zl, 14, sib))
            self.l[2].wait_recv()
            self.s.append(self.on(2, zl, 15, sib))

        def end(self):
            for cp in self.s:
                cp.wait_recv()

    qy = Round(
        qw.at[c * 2 + zl, pl.ds(512 + y * 128, 128)],
        lambda h, cc, cy, p: wq.at[h * 4 + cc * 2 + p, pl.ds(512 + cy * 128, 128)], ys, yrr,
    )

    rows_mine = pl.ds(c * 2048 + zl * 1024, 1024)
    rows_there = pl.ds(zh * 4096 + c * 2048 + zl * 1024, 1024)
    k1 = [
        go(send(kw.at[rows_mine], wkv.at[rows_there, pl.ds(0, 128)], ks.at[0], kr.at[0], cross)),
        go(send(vw.at[rows_mine], wkv.at[rows_there, pl.ds(128, 128)], ks.at[1], kr.at[1], cross)),
    ]

    class Pair:
        def __init__(self, sources, piece, ss, rr):
            self.piece, self.ss, self.rr = piece, ss, rr
            self.first = [
                go(send(src, piece(zh, c, zl, j), ss.at[0, j], rr.at[0, j], cross)) for j, src in enumerate(sources)
            ]
            self.near, self.s = {}, []

        def crossed(self, j):
            self.first[j].wait_recv()
            piece = self.piece(1 - zh, c, 1 - zl, j)
            self.near[j] = go(send(piece, piece, self.ss.at[1, j], self.rr.at[1, j], near))
            self.s.append(go(send(piece, piece, self.ss.at[2, j], self.rr.at[2, j], sib)))

        def neared(self, j):
            self.near[j].wait_recv()
            piece = self.piece(1 - zh, c, zl, j)
            self.s.append(go(send(piece, piece, self.ss.at[3, j], self.rr.at[3, j], sib)))

        def end(self):
            for cp in self.s:
                cp.wait_recv()

    def wq_at(h, cc, p, j):
        return wq.at[h * 4 + cc * 2 + p, pl.ds(j * 256, 256)]

    q1 = [
        go(send(qw.at[c * 2 + zl, pl.ds(j * 256, 256)], wq_at(zh, c, zl, j), qs.at[0, j], qr.at[0, j], cross))
        for j in range(2)
    ]

    local[0].wait()
    lanes = jnp.zeros((256, 128), F32)
    for j in range(16):
        t = raw[:, j * 128 : (j + 1) * 128].astype(F32)
        lanes = lanes + t * t
    row = jnp.sum(lanes.T, axis=0, keepdims=True)
    sums[x] = jnp.broadcast_to(row, (8, 256))
    s_cp = [
        go(send(sums.at[x], sums.at[x], sum_s.at[d - 1], sum_r.at[d - 1], {"image": (x + d) % 4}))
        for d in (1, 2, 3)
    ]
    for n in (1, 2, 3):
        p_first(n)

    def p_relay(n):
        p_r[n].wait_recv()
        p_r.append(go(send(prow(xl, n), prow(xl, n), ps.at[4 + n], pr.at[4 + n], right)))
        p_l[n].wait_recv()
        i = 3 - n
        p_l.append(go(send(prow(xr, i), prow(xr, i), ps.at[10 + n], pr.at[10 + n], left)))

    qy.crossed()
    p_relay(0)
    for cp in s_cp:
        cp.wait_recv()
    total = sums[0] + sums[1] + sums[2] + sums[3]
    inv = lax.rsqrt(total[0:1] * (1.0 / D) + EPS)
    inv = jnp.broadcast_to(inv, (128, 256)).T
    for j in range(16):
        t = raw[:, j * 128 : (j + 1) * 128].astype(F32)
        g = gain[pl.ds(x * 16 + j, 1), :]
        tn[x, :, j * 128 : (j + 1) * 128] = (t * inv * g).astype(BF16)

    def trow(slot, b, half):
        return tn.at[slot, pl.ds(b * BLOCK + half * HALF, HALF)]

    t_r, t_l = [[], []], [[], []]

    def t_first(b):
        for n in (0, 1):
            piece = trow(x, b, n)
            t_r[b].append(go(send(piece, piece, ts.at[b, n], tr.at[b, n], right)))
            piece = trow(x, b, 1 - n)
            t_l[b].append(go(send(piece, piece, ts.at[b, 3 + n], tr.at[b, 3 + n], left)))

    def t_relay(b):
        t_r[b][0].wait_recv()
        piece = trow(xl, b, 0)
        t_r[b].append(go(send(piece, piece, ts.at[b, 2], tr.at[b, 2], right)))
        t_l[b][0].wait_recv()
        piece = trow(xr, b, 1)
        t_l[b].append(go(send(piece, piece, ts.at[b, 5], tr.at[b, 5], left)))

    def wkv_at(cc, p, v):
        return wkv.at[pl.ds((1 - zh) * 4096 + cc * 2048 + p * 1024, 1024), pl.ds(v * 128, 128)]

    p_relay(1)
    t_first(0)
    qy.neared()
    k2, k3 = [], []
    for v in (0, 1):
        k1[v].wait_recv()
        piece = wkv_at(c, 1 - zl, v)
        k2.append(go(send(piece, piece, ks.at[2 + v], kr.at[2 + v], near)))
        k3.append(go(send(piece, piece, ks.at[4 + v], kr.at[4 + v], sib)))
    qy.y_first()
    qy.y_second()
    for v in (0, 1):
        k2[v].wait_recv()
        piece = wkv_at(c, zl, v)
        k3.append(go(send(piece, piece, ks.at[6 + v], kr.at[6 + v], sib)))

    q2, q3 = [], []

    def q_pass(j):
        q1[j].wait_recv()
        piece = wq_at(1 - zh, c, 1 - zl, j)
        q2.append(go(send(piece, piece, qs.at[1, j], qr.at[1, j], near)))
        q3.append(go(send(piece, piece, qs.at[2, j], qr.at[2, j], sib)))

    def q_last(j):
        q2[j].wait_recv()
        piece = wq_at(1 - zh, c, zl, j)
        q3.append(go(send(piece, piece, qs.at[3, j], qr.at[3, j], sib)))

    q_pass(0)

    for cp in p_r[2:] + p_l[2:] + k3:
        cp.wait_recv()
    for i in (1, 2, 3):
        local[i].wait()
    kvacc[...] = jnp.zeros_like(kvacc)

    def kv_step(i, carry):
        cols = pl.ds(pl.multiple_of(i * 1024, 1024), 1024)
        kvacc[...] += jnp.dot(pb[:, cols], wkv[cols, :], preferred_element_type=F32)
        return carry

    lax.fori_loop(0, 8, kv_step, 0)

    def block(dy, dz):
        sc, sd = at(-dy, -dz)
        return kvb.at[sc * 2 + sd]

    mine = ctx * 2 + zh
    kvb[mine, :, 0:128] = rms(kvacc[:, 0:128], kg[...]).astype(BF16)
    kvb[mine, :, 128:256] = kvacc[:, 128:256].astype(BF16)
    g_cp, h_cp = {}, []

    def g_send(sy, sz, dy, dz):
        piece, k = block(sy, sz), (sy + dy) * 4 + sz + dz
        g_cp[k] = go(send(piece, piece, gs.at[k], gr.at[k], to(dy, dz)))

    def h_send(sy, sz):
        piece, k = block(sy, sz), sy * 4 + sz
        h_cp.append(go(send(piece, piece, hs.at[k], hr.at[k], sib)))

    for dz in (1, 3, 2):
        g_send(0, 0, 0, dz)
    for dy in (1, 3):
        g_send(0, 0, dy, 0)
    h_send(0, 0)

    t_relay(0)
    t_first(1)
    qy.y_far()
    for dz in (1, 3, 2):
        g_cp[dz].wait_recv()
        for dy in (1, 3):
            g_send(0, dz, dy, 0)
        h_send(0, dz)
    oy = Round(
        ow.at[pl.ds(c * 512 + zl * 256 + 128 + y * 32, 32)],
        lambda h, cc, cy, p: wo.at[pl.ds(cc * 512 + p * 256 + 128 + cy * 32, 32)], os, orr,
    )
    oz = Pair(
        [ow.at[pl.ds(c * 512 + zl * 256 + j * 64, 64)] for j in (0, 1)],
        lambda h, cc, p, j: wo.at[pl.ds(cc * 512 + p * 256 + j * 64, 64)], zs, zr,
    )
    q_last(0)
    q_pass(1)
    for dz in (0, 1, 3, 2):
        for dy in (1, 3):
            g_cp[dy * 4 + dz].wait_recv()
            if (dy == 1) == (dz < 2):
                g_send(dy, dz, (2 - dy), 0)
            h_send(dy, dz)
    t_relay(1)
    q_last(1)
    oy.crossed()

    def project(slot, b):
        def step(i, carry):
            cols = pl.ds(pl.multiple_of(i * 512, 512), 512)
            rows = pl.ds(pl.multiple_of((i % 2) * 512, 512), 512)
            acc[...] += jnp.dot(
                tn[slot, b * BLOCK : (b + 1) * BLOCK, cols], wq[slot * 2 + i // 2, rows, :],
                preferred_element_type=F32,
            )
            return carry

        lax.fori_loop(0, 4, step, 0)

    def queries(b):
        acc[...] = jnp.zeros_like(acc)
        project(x, b)
        t_r[b][1].wait_recv()
        project(xl, b)
        t_l[b][1].wait_recv()
        project(xr, b)
        t_r[b][2].wait_recv()
        t_l[b][2].wait_recv()
        project(xo, b)
        for h in range(8):
            v = rms(acc[:, h * HD : (h + 1) * HD], qg[...])
            qh[b, h * BLOCK : (h + 1) * BLOCK, :] = v.astype(BF16)

    local[4].wait()
    for cp in q3:
        cp.wait_recv()
    qy.end()
    queries(0)
    oz.crossed(0)
    for dz in (0, 1, 3, 2):
        g_cp[8 + dz].wait_recv()
        h_send(2, dz)
    oy.neared()
    for cp in h_cp:
        cp.wait_recv()

    def attend(b, lo, hi):
        if lo == 0:
            m[...] = jnp.full_like(m, -1e30)
            l[...] = jnp.zeros_like(l)
            a[...] = jnp.zeros_like(a)

        def step(s, carry):
            valid = mask[b, owner[s]]
            rows_s = pl.ds(pl.multiple_of(s * 32, 32), 32)

            def scores(t):
                keys = kvb[:, rows_s, 0:128].reshape(1024, 128)
                return lax.dot_general(
                    qh[b, t * 256 : (t + 1) * 256, :], keys, (((1,), (1,)), ((), ())),
                    preferred_element_type=F32,
                )

            after = scores(0)
            for t in range(4):
                rows = slice(t * 256, (t + 1) * 256)
                sc = after
                if t < 3:
                    after = scores(t + 1)
                old = m[rows, :]
                top = jnp.max(sc, axis=-1, keepdims=True) * SCALE
                new = jnp.where(valid > 0, jnp.maximum(old, top), old)
                low = jnp.where(valid > 0, new, 1e30)
                w = jnp.exp2(sc * SCALE - low[:, 0:1])
                fac = jnp.exp2(old - new)
                vals = kvb[:, rows_s, 128:256].reshape(1024, 128)
                l[rows, :] = l[rows, :] * fac + jnp.sum(w, axis=-1, keepdims=True)
                a[rows, :] = a[rows, :] * fac + jnp.dot(w.astype(BF16), vals, preferred_element_type=F32)
                m[rows, :] = new
            return carry

        lax.fori_loop(lo, hi, step, 0)
        if hi == 8:
            for h in range(8):
                rows = slice(h * BLOCK, (h + 1) * BLOCK)
                att[b, :, h * HD : (h + 1) * HD] = (a[rows, :] / l[rows, :]).astype(BF16)

    def give_to(b, i):
        return send(give.at[b, i], take.at[b, i], rs.at[b, i], rr.at[b, i], left if i in (1, 4, 5) else right)

    r_cp = [{}, {}]

    def product(b, t, store):
        def step(n, carry):
            cols = pl.ds(pl.multiple_of((n % 2) * 512, 512), 512)
            v = jnp.dot(att[b], wq[t * 2 + n // 2, :, cols], preferred_element_type=F32)
            store(pl.ds(pl.multiple_of(n * 512, 512), 512), v)
            return carry

        lax.fori_loop(0, 4, step, 0)

    def reduce_start(b):
        def far(cols, v):
            give[b, 0, :, cols] = v[0:HALF].astype(BF16)
            give[b, 1, :, cols] = v[HALF:BLOCK].astype(BF16)

        def to_right(cols, v):
            give[b, 3, :, cols] = v[HALF:BLOCK].astype(BF16)
            part[b, 0, :, cols] = v[0:HALF]

        def to_left(cols, v):
            give[b, 4, :, cols] = v[0:HALF].astype(BF16)
            part[b, 1, :, cols] = v[HALF:BLOCK]

        for t, store, slots in ((xo, far, (0, 1)), (xr, to_right, (3,)), (xl, to_left, (4,))):
            product(b, t, store)
            for i in slots:
                r_cp[b][i] = go(give_to(b, i))

    def reduce_relay(b):
        for k, i in ((0, 2), (1, 5)):
            r_cp[b][k].wait_recv()
            give[b, i] = (part[b, k] + take[b, k].astype(F32)).astype(BF16)
            r_cp[b][i] = go(give_to(b, i))

    def own_product(b):
        def store(cols, v):
            part[b, 0, :, cols] = v[0:HALF]
            part[b, 1, :, cols] = v[HALF:BLOCK]

        product(b, x, store)

    def finish(b):
        scale = jnp.tanh(jnp.full((8, 128), gate[0], F32))[0:1, 0:1]
        for k, (i, j) in enumerate(((4, 2), (3, 5))):
            r_cp[b][i].wait_recv()
            r_cp[b][j].wait_recv()
            v = part[b, k] + take[b, i].astype(F32) + take[b, j].astype(F32)
            out[b * BLOCK + k * HALF : b * BLOCK + (k + 1) * HALF] = (scale * v).astype(BF16)

    oz.crossed(1)
    attend(0, 0, 2)
    oy.y_first()
    oy.y_second()
    attend(0, 2, 4)
    oz.neared(0)
    oy.y_far()
    queries(1)
    oz.neared(1)
    attend(0, 4, 8)
    oy.end()
    oz.end()
    for cp in sends:
        cp.wait_send()
    sends.clear()
    loads = []
    for i in range(4):
        cols = pl.ds(i * 1024, 1024)
        loads.append(pltpu.make_async_copy(ow.at[:, cols], wq.at[zh * 4 + i], wload.at[i]))
        loads.append(pltpu.make_async_copy(wo.at[:, cols], wq.at[(1 - zh) * 4 + i], wload.at[4 + i]))
    for cp in loads:
        cp.start()
    attend(1, 0, 2)
    for cp in loads:
        cp.wait()
    reduce_start(0)
    attend(1, 2, 5)
    reduce_relay(0)
    own_product(0)
    attend(1, 5, 8)
    reduce_start(1)
    finish(0)
    reduce_relay(1)
    own_product(1)
    finish(1)
    for cp in sends:
        cp.wait_send()


def local(
    text, patches, in_gain, q_weight, k_weight, v_weight, o_weight, q_gain, k_gain, gate, block_mask, owner_ids
):
    dma = pltpu.SemaphoreType.DMA
    smem = pl.BlockSpec(memory_space=pltpu.SMEM)
    return pl.pallas_call(
        kernel,
        name="gated_cross_attention",
        out_shape=jax.ShapeDtypeStruct((256, 2048), BF16),
        in_specs=[ANY, ANY, VMEM, ANY, ANY, ANY, ANY, VMEM, VMEM, smem, smem, smem],
        out_specs=VMEM,
        scratch_shapes=[
            pltpu.VMEM((1024, 4096), BF16),
            pltpu.VMEM((256, 2048), BF16),
            pltpu.VMEM((4, 256, 2048), BF16),
            pltpu.VMEM((256, D), BF16),
            pltpu.VMEM((8, 1024, 1024), BF16),
            pltpu.VMEM((D, 256), BF16),
            pltpu.VMEM((BLOCK, 1024), F32),
            pltpu.VMEM((256, 256), F32),
            pltpu.VMEM((32, 256, 256), BF16),
            pltpu.VMEM((4, 8, 256), F32),
            pltpu.VMEM((2, 1024, HD), BF16),
            pltpu.VMEM((1024, HD), F32),
            pltpu.VMEM((1024, HD), F32),
            pltpu.VMEM((1024, HD), F32),
            pltpu.VMEM((2, BLOCK, 1024), BF16),
            pltpu.VMEM((2, 2, HALF, 2048), F32),
            pltpu.VMEM((2, 6, HALF, 2048), BF16),
            pltpu.VMEM((2, 6, HALF, 2048), BF16),
            dma((5,)), dma((8,)), dma((3,)), dma((3,)), dma((12,)), dma((12,)), dma((2, 6)), dma((2, 6)),
            dma((8,)), dma((8,)), dma((4, 2)), dma((4, 2)), dma((16,)), dma((16,)), dma((4, 2)), dma((4, 2)), dma((16,)), dma((16,)),
            dma((16,)), dma((16,)), dma((16,)), dma((16,)), dma((2, 6)), dma((2, 6)),
        ],
        compiler_params=pltpu.CompilerParams(
            collective_id=0, has_side_effects=True, vmem_limit_bytes=60 << 20
        ),
    )(
        text, patches.reshape(64, D), in_gain.reshape(64, 128), q_weight.reshape(4, 1024, 1024), k_weight, v_weight,
        o_weight, q_gain.reshape(1, HD), k_gain.reshape(1, HD), gate, block_mask, owner_ids,
    )


def solution(mesh):
    in_specs = (
        P(("context", "dp"), "image"),
        P("image", ("context", "dp"), None),
        P(),
        P("dp", "image"),
        P("dp", "image"),
        P("dp", "image"),
        P("image", "dp"),
        P(),
        P(),
        P(),
        P(("context", "dp"), None),
        P(),
    )
    out_specs = P(("context", "dp"), "image")
    return jax.shard_map(local, mesh=mesh, in_specs=in_specs, out_specs=out_specs, check_vma=False)
```
